32 devices in a mesh: lon: 4 (over y, x), lat: 8 (over z, core).
Axes of the slice: x: 2, y: 2, z: 4, core: 2. Of those that a mesh axis runs over, the one named last changes fastest.
Arguments:
- prognostic: bfloat16 [7, 8, 128, 2048], P(None, None, 'lat', 'lon'), may hold values from -6 to 6
- halo_depth: int32 [2, 8, 4], P(None, 'lat', 'lon'), may hold values from 3 to 10, as said below
- cell_offsets: int32 [2, 8, 128, 2048], P(None, None, 'lat', 'lon'), may hold values from -8 to 8, as said below
Outputs:
- advected: bfloat16 [7, 8, 128, 2048], P(None, None, 'lat', 'lon')
The draws below stay inside these ranges and needn't reach their ends.
Inputs may be any that keep to these rules, and one draw needn't show every extreme that they name: `halo_depth`: every depth is 3 or more; row depths are at most 10, column depths at most 8; some tile has row depth 10 and column depth 8. |cell_offsets[0]| <= (its tile's row depth) - 2 and |cell_offsets[1]| <= (its tile's column depth) - 2; row y + cell_offsets[0] lies in 0 to 126.
All inputs are finite; a program needn't handle non-finite values.
Results may differ from the reference program's by a relative error of at most 0.0047.
Values may be sent and summed in bfloat16 or wider, within the bound.
A program may use at most 64 MiB of HBM per device.

```python
import math
import jax
import jax.numpy as jnp
from jax import lax

NFIELD = 7
LEV = 8
CLAT = 16
CLON = 512
HO = 8
HL = 10
ITERS = 3
NLAT = 128
NLON = 2048
N_LON = 4
N_LAT = 8


def depth_grid(key):
    base_key = jax.random.fold_in(key, 101)
    row_depths = jax.random.randint(jax.random.fold_in(base_key, 1), (N_LAT, N_LON), 3, HL + 1)
    col_depths = jax.random.randint(jax.random.fold_in(base_key, 2), (N_LAT, N_LON), 3, HO + 1)
    row_depths = row_depths.at[N_LAT // 2, 0].set(HL).at[0, 0].set(3)
    col_depths = col_depths.at[N_LAT // 2, 0].set(HO).at[0, 0].set(3)
    return jnp.stack([row_depths, col_depths]).astype(jnp.int32)


def draw_halo_depth(key, part):
    return depth_grid(key)


def draw_cell_offsets(key, part):
    grid_depth = depth_grid(key)
    rows_depth = jnp.repeat(jnp.repeat(grid_depth[0], CLAT, axis=0), CLON, axis=1)
    cols_depth = jnp.repeat(jnp.repeat(grid_depth[1], CLAT, axis=0), CLON, axis=1)
    lat_row = jnp.arange(NLAT, dtype=jnp.int32)[:, None]
    lat_low = jnp.maximum(2 - rows_depth, 0 - lat_row)
    lat_high = jnp.minimum(rows_depth - 2, NLAT - 2 - lat_row)
    grid_shape = (LEV, NLAT, NLON)
    row_off = jax.random.randint(jax.random.fold_in(key, 3), grid_shape, lat_low[None], lat_high[None] + 1)
    col_off = jax.random.randint(jax.random.fold_in(key, 4), grid_shape, 2 - cols_depth[None], cols_depth[None] - 1)
    centre = N_LAT // 2 * CLAT
    row_off = row_off.at[0, centre, 0].set(HL - 2).at[0, centre, 1].set(2 - HL)
    col_off = col_off.at[0, centre, 0].set(HO - 2).at[0, centre, 1].set(2 - HO)
    return jnp.stack([row_off, col_off]).astype(jnp.int32)


def levels(own_key, extent, split, least, high):
    gain, own = 1.0, jax.random.fold_in(own_key, 6)
    for position, parts in split:
        heights = jnp.exp(jax.random.uniform(jax.random.fold_in(own, position), (parts,), jnp.float32, least / len(split), high / len(split)))
        gain = gain * jnp.repeat(heights, extent[position] // parts).reshape([-1 if axis == position else 1 for axis in range(len(extent))])
    return gain


def bell_draw(rng, extent, scale, limit, cuts=(), kind=jnp.bfloat16):
    result = jax.random.normal(rng, extent, jnp.float32) * scale
    if len(cuts) > 0:
        result = levels(rng, extent, cuts, -0.22, 0.18) * result
    return jnp.clip(result, min=-limit, max=limit).astype(kind)


def setup_inputs(seed: int = 0) -> dict:
    streams_of = jax.random.split(jax.random.key(seed), 4)
    prognostic = bell_draw(streams_of[0], (NFIELD, LEV, NLAT, NLON), 1.0, 6.0, ((2, 8), (3, 4)))
    halo_depth = draw_halo_depth(jax.random.fold_in(streams_of[3], 71), 0)
    cell_offsets = draw_cell_offsets(jax.random.fold_in(streams_of[3], 71), 0)
    return dict(prognostic=prognostic, halo_depth=halo_depth, cell_offsets=cell_offsets)


courant = 2.0


def keys_kernel(offset):
    magnitude = jnp.abs(offset)
    near_part = (1.5 * magnitude - 2.5) * magnitude * magnitude + 1.0
    far_part = ((-0.5 * magnitude + 2.5) * magnitude - 4.0) * magnitude + 2.0
    return jnp.where(magnitude <= 1.0, near_part, jnp.where(magnitude < 2.0, far_part, 0.0))


def pad_fields(fields):
    wrapped = jnp.concatenate([fields[:, :, NLON - HO:], fields, fields[:, :, :HO]], axis=2)
    return jnp.pad(wrapped, ((0, 0), (HL, HL), (0, 0)))


def sample(padded, row_off, row_frac, col_off, col_frac):
    lat_rows = jnp.arange(NLAT, dtype=jnp.int32)[:, None] + (HL - 1) + row_off
    lon_cols = jnp.arange(NLON, dtype=jnp.int32)[None, :] + (HO - 1) + col_off
    summed = jnp.zeros((padded.shape[0], NLAT, NLON), jnp.float32)
    for row_tap in range(4):
        row_weight = keys_kernel((row_tap - 1.0) - row_frac)
        along = jnp.zeros((padded.shape[0], NLAT, NLON), jnp.float32)
        for col_tap in range(4):
            col_weight = keys_kernel((col_tap - 1.0) - col_frac).astype(jnp.bfloat16)
            col_weight = lax.optimization_barrier(col_weight).astype(jnp.float32)
            picked = padded[:, lat_rows + row_tap, lon_cols + col_tap].astype(jnp.float32)
            along = along + col_weight * picked
        summed = summed + row_weight * along
    return summed


def trajectory(wind_pad, row_off, col_off, rows_depth, cols_depth, coslat):
    row_frac = jnp.full(row_off.shape, 0.5, jnp.float32)
    col_frac = jnp.full(col_off.shape, 0.5, jnp.float32)
    row_mid = jnp.floor_divide(row_off, 2)
    col_mid = jnp.floor_divide(col_off, 2)
    row_float = row_off.astype(jnp.float32)
    col_float = col_off.astype(jnp.float32)
    for repeat in range(ITERS):
        row_part = ((row_off - 2 * row_mid).astype(jnp.float32) + row_frac) * 0.5
        col_part = ((col_off - 2 * col_mid).astype(jnp.float32) + col_frac) * 0.5
        mid_wind = sample(wind_pad, row_mid, row_part, col_mid, col_part)
        lon_reach = -courant * mid_wind[0] / coslat
        lat_reach = -courant * mid_wind[1]
        lon_limit = (cols_depth - 1.0) * jnp.tanh(lon_reach / (cols_depth - 1.0))
        lat_limit = (rows_depth - 1.0) * jnp.tanh(lat_reach / (rows_depth - 1.0))
        row_frac = 0.5 + 0.5 * jnp.tanh(0.5 * (lat_limit - row_float - 0.5))
        col_frac = 0.5 + 0.5 * jnp.tanh(0.5 * (lon_limit - col_float - 0.5))
    return row_frac, col_frac


def reference(prognostic, halo_depth, cell_offsets):
    rows_depth = jnp.repeat(jnp.repeat(halo_depth[0], CLAT, axis=0), CLON, axis=1).astype(jnp.float32)
    cols_depth = jnp.repeat(jnp.repeat(halo_depth[1], CLAT, axis=0), CLON, axis=1).astype(jnp.float32)
    lat_index = jnp.arange(NLAT, dtype=jnp.int32).astype(jnp.float32)
    coslat = jnp.cos((lat_index + 0.5) * (math.pi / NLAT) - 0.5 * math.pi)[:, None]

    def one_level(level_index):
        fields = lax.dynamic_index_in_dim(prognostic, level_index, 1, keepdims=False)
        offsets_level = lax.dynamic_index_in_dim(cell_offsets, level_index, 1, keepdims=False)
        padded = pad_fields(fields)
        row_off = offsets_level[0]
        col_off = offsets_level[1]
        row_frac, col_frac = trajectory(padded[0:2], row_off, col_off, rows_depth, cols_depth, coslat)
        return sample(padded, row_off, row_frac, col_off, col_frac).astype(jnp.bfloat16)

    advected = lax.map(one_level, jnp.arange(LEV, dtype=jnp.int32))
    return jnp.moveaxis(advected, 0, 1)
```

```python
import functools
import math

import jax
import jax.numpy as jnp
from jax import lax
from jax.experimental import pallas as pl
from jax.experimental.pallas import tpu as pltpu
from jax.sharding import PartitionSpec as P

HO = 8
HL = 10
ITERS = 3
STEP = 104
LANES = 128
courant = 2.0


def passed_along(value, axis, by):
    devices = lax.axis_size(axis)
    pairs = [(i, i + by) for i in range(devices) if 0 <= i + by < devices]
    return lax.ppermute(value, axis, pairs)


def from_behind(value, axis, steps):
    count = lax.axis_size(axis)
    pairs = [(source, (source + steps) % count) for source in range(count)]
    return lax.ppermute(value, axis, pairs)


def far(m):
    return ((-0.5 * m + 2.5) * m - 4.0) * m + 2.0


def near(m):
    return (1.5 * m - 2.5) * m * m + 1.0


def tap_weights(g):
    return [far(1.0 + g), near(g), near(1.0 - g), far(2.0 - g)]


def col_weights(h):
    w = [v.astype(jnp.bfloat16).astype(jnp.float32) for v in tap_weights(h)]
    tiny = 1.0 / 65536.0
    return [w[0], w[1] - w[0] * tiny, w[2], w[3] - w[2] * tiny]


def classes(start):
    groups = [(start + (3 - k)) >> 2 for k in range(4)]
    taps = [(groups[k] << 2) + k - start for k in range(4)]
    return groups, taps


def class_weights(taps, g):
    w = tap_weights(g)
    return [
        jnp.where(t == 0, w[0], jnp.where(t == 1, w[1], jnp.where(t == 2, w[2], w[3])))
        for t in taps
    ]


def window(parts, first, lane):
    block, off = divmod(first, LANES)
    if off == 0:
        return parts(block)
    a = pltpu.roll(parts(block), LANES - off, 1)
    b = pltpu.roll(parts(block + 1), LANES - off, 1)
    return jnp.where(lane < LANES - off, a, b)


def pick(table, idx):
    return jnp.take_along_axis(table, idx, axis=1, mode="promise_in_bounds")


def kernel(factor_ref, ext_ref, off_ref, out_ref, words, offs, inv, res):
    fields, rows_ext, levels, _ = ext_ref.shape
    _, rows, _, cols = out_ref.shape
    count = words.shape[2]
    lane = lax.broadcasted_iota(jnp.int32, (levels, LANES), 1)
    blocks = cols // LANES + 2

    def block_of(ref, *lead):
        return lambda i: ref[(*lead, slice(None), slice(i * LANES, (i + 1) * LANES))]

    for f in range(fields):
        def biggest(r, top):
            for i in range(blocks):
                top = jnp.maximum(top, jnp.abs(block_of(ext_ref, f, r)(i).astype(jnp.float32)))
            return top

        top = lax.fori_loop(0, rows_ext, biggest, jnp.zeros((levels, LANES), jnp.float32))
        top = jnp.maximum(jnp.max(top, axis=1, keepdims=True), 1e-30)
        power = jnp.floor(jnp.log(32000.0 / top) * (1.0 / math.log(2.0)))
        scale = jnp.broadcast_to(jnp.exp(power * math.log(2.0)), (levels, LANES))
        inv[f] = (1.0 / 65536.0) / scale

        def pack(r, _):
            def quantized(i):
                v = block_of(ext_ref, f, r)(i).astype(jnp.float32)
                return jnp.floor(v * scale + 0.5).astype(jnp.int32)

            memo = {}

            def part(i):
                if i not in memo:
                    memo[i] = quantized(i)
                return memo[i]

            for j in range(count):
                q = window(part, LANES - HO + STEP * j, lane)
                words[f, r, j] = (q << 16) + pltpu.roll(q, LANES - 1, 1)
            return 0

        lax.fori_loop(0, rows_ext, pack, 0)

    def windows_of(y, _):
        for c in range(2):
            for j in range(count):
                offs[c, y, j] = window(block_of(off_ref, c, y), LANES - HO + STEP * j, lane)
        return 0

    lax.fori_loop(0, rows, windows_of, 0)

    sy, dy, dx = factor_ref[rows], factor_ref[rows + 1], factor_ref[rows + 2]

    def stencil(f, row, j, idx, groups, masks, k, p):
        value = pick(words[f, row + k, j], idx[p])
        for g in range(1, groups):
            value = jnp.where(masks[k][g - 1], pick(words[f, row + 4 * g + k, j], idx[p]), value)
        return value.astype(jnp.float32), (value << 16).astype(jnp.float32)

    def point(i, _):
        y = i // count
        j = i - y * count
        oy = offs[0, y, j]
        ox = offs[1, y, j]
        oyf = oy.astype(jnp.float32)
        oxf = ox.astype(jnp.float32)
        my = oy >> 1
        mx = ox >> 1
        idx = [(lane + mx + (2 * p - 1)) & (LANES - 1) for p in range(2)]
        groups, taps = classes(my + 4)
        masks = [[groups[k] >= g for g in (1, 2)] for k in range(4)]
        wind = [
            [
                [v for p in range(2) for v in stencil(f, y + 5, j, idx, 3, masks, k, p)]
                for k in range(4)
            ]
            for f in range(2)
        ]
        sx = factor_ref[y]
        odd_y = (oy & 1).astype(jnp.float32)
        odd_x = (ox & 1).astype(jnp.float32)
        fy = jnp.full(oy.shape, 0.5, jnp.float32)
        fx = fy
        for _ in range(ITERS):
            cw = col_weights((odd_x + fx) * 0.5)
            rw = class_weights(taps, (odd_y + fy) * 0.5)
            mid = []
            for f in range(2):
                total = 0.0
                for k in range(4):
                    v = wind[f][k]
                    total += rw[k] * (cw[0] * v[0] + cw[1] * v[1] + cw[2] * v[2] + cw[3] * v[3])
                mid.append(total * inv[f])
            lx = dx * jnp.tanh(mid[0] * sx)
            ly = dy * jnp.tanh(mid[1] * sy)
            fy = 0.5 + 0.5 * jnp.tanh(0.5 * (ly - oyf - 0.5))
            fx = 0.5 + 0.5 * jnp.tanh(0.5 * (lx - oxf - 0.5))

        idx = [(lane + ox + (2 * p - 1)) & (LANES - 1) for p in range(2)]
        groups, taps = classes(oy + 8)
        masks = [[groups[k] >= g for g in (1, 2, 3, 4)] for k in range(4)]
        cw = col_weights(fx)
        rw = class_weights(taps, fy)
        for f in range(fields):
            total = 0.0
            for k in range(4):
                a = stencil(f, y + 1, j, idx, 5, masks, k, 0)
                b = stencil(f, y + 1, j, idx, 5, masks, k, 1)
                total += rw[k] * (cw[0] * a[0] + cw[1] * a[1] + cw[2] * b[0] + cw[3] * b[1])
            res[f, y, j] = total * inv[f]
        return 0

    lax.fori_loop(0, rows * count, point, 0)

    def merge(y, _):
        for f in range(fields):
            for m in range(cols // LANES):
                begin = m * LANES
                out = None
                for j in range(begin // STEP, (begin + LANES - 1) // STEP + 1):
                    moved = pltpu.roll(res[f, y, j], (STEP * j - HO - begin) % LANES, 1)
                    out = moved if out is None else jnp.where(lane >= STEP * j - begin, moved, out)
                out_ref[f, y, :, begin : begin + LANES] = out.astype(out_ref.dtype)
        return 0

    lax.fori_loop(0, rows, merge, 0)


def extend(fields):
    f, rows, levels, cols = fields.shape
    below = passed_along(fields[:, rows - HL :], "lat", 1)
    above = passed_along(fields[:, :HL], "lat", -1)
    tall = jnp.concatenate([below, fields, above], axis=1)
    count = rows + 2 * HL
    west_edge = jnp.moveaxis(tall[..., :HO], 3, 0).reshape(HO, f * count * levels)
    east_edge = jnp.moveaxis(tall[..., cols - HO :], 3, 0).reshape(HO, f * count * levels)
    west = from_behind(east_edge, "lon", 1).reshape(HO, f, count, levels)
    east = from_behind(west_edge, "lon", -1).reshape(HO, f, count, levels)
    blank = jnp.zeros((f, count, levels, LANES - HO), fields.dtype)
    return jnp.concatenate(
        [blank, jnp.moveaxis(west, 0, 3), tall, jnp.moveaxis(east, 0, 3), blank], axis=3
    )


def on_device(prognostic, halo_depth, cell_offsets):
    fields, levels, rows, cols = prognostic.shape
    ext = extend(jnp.transpose(prognostic, (0, 2, 1, 3)))
    off = jnp.pad(
        jnp.transpose(cell_offsets, (0, 2, 1, 3)), ((0, 0), (0, 0), (0, 0), (LANES, LANES))
    )
    lat_total = rows * lax.axis_size("lat")
    lat_index = (lax.axis_index("lat") * rows + jnp.arange(rows, dtype=jnp.int32)).astype(jnp.float32)
    coslat = jnp.cos((lat_index + 0.5) * (math.pi / lat_total) - 0.5 * math.pi)
    depth = halo_depth[:, 0, 0].astype(jnp.float32) - 1.0
    factor = jnp.concatenate(
        [-courant / (coslat * depth[1]), (-courant / depth[0])[None], depth]
    )
    count = -(-cols // STEP)
    moved = pl.pallas_call(
        kernel,
        out_shape=jax.ShapeDtypeStruct((fields, rows, levels, cols), jnp.bfloat16),
        in_specs=[
            pl.BlockSpec(memory_space=pltpu.SMEM),
            pl.BlockSpec(memory_space=pltpu.VMEM),
            pl.BlockSpec(memory_space=pltpu.VMEM),
        ],
        out_specs=pl.BlockSpec(memory_space=pltpu.VMEM),
        scratch_shapes=[
            pltpu.VMEM((fields, rows + 2 * HL, count, levels, LANES), jnp.int32),
            pltpu.VMEM((2, rows, count, levels, LANES), jnp.int32),
            pltpu.VMEM((fields, levels, LANES), jnp.float32),
            pltpu.VMEM((fields, rows, count, levels, LANES), jnp.float32),
        ],
        compiler_params=pltpu.CompilerParams(vmem_limit_bytes=40 * 2**20),
    )(factor, ext, off)
    return jnp.transpose(moved, (0, 2, 1, 3))


def solution(mesh):
    in_specs = (P(None, None, "lat", "lon"), P(None, "lat", "lon"), P(None, None, "lat", "lon"))
    out_specs = P(None, None, "lat", "lon")
    return jax.shard_map(
        on_device, mesh=mesh, in_specs=in_specs, out_specs=out_specs, check_vma=False
    )
```

```python
import functools
import math

import jax
import jax.numpy as jnp
from jax import lax
from jax.experimental import pallas as pl
from jax.experimental.pallas import tpu as pltpu
from jax.sharding import PartitionSpec as P

HO = 8
HL = 10
ITERS = 3
STEP = 104
LANES = 128
courant = 2.0


def passed_along(value, axis, by):
    devices = lax.axis_size(axis)
    pairs = [(i, i + by) for i in range(devices) if 0 <= i + by < devices]
    return lax.ppermute(value, axis, pairs)


def from_behind(value, axis, steps):
    count = lax.axis_size(axis)
    pairs = [(source, (source + steps) % count) for source in range(count)]
    return lax.ppermute(value, axis, pairs)


def far(m):
    return ((-0.5 * m + 2.5) * m - 4.0) * m + 2.0


def near(m):
    return (1.5 * m - 2.5) * m * m + 1.0


def tap_weights(g):
    return [far(1.0 + g), near(g), near(1.0 - g), far(2.0 - g)]


def col_weights(h):
    w = [v.astype(jnp.bfloat16).astype(jnp.float32) for v in tap_weights(h)]
    tiny = 1.0 / 65536.0
    return [w[0], w[1] - w[0] * tiny, w[2], w[3] - w[2] * tiny]


def classes(start):
    groups = [(start + (3 - k)) >> 2 for k in range(4)]
    taps = [(groups[k] << 2) + k - start for k in range(4)]
    return groups, taps


def class_weights(taps, g):
    w = tap_weights(g)
    return [
        jnp.where(t == 0, w[0], jnp.where(t == 1, w[1], jnp.where(t == 2, w[2], w[3])))
        for t in taps
    ]


def window(parts, first, lane):
    block, off = divmod(first, LANES)
    if off == 0:
        return parts(block)
    a = pltpu.roll(parts(block), LANES - off, 1)
    b = pltpu.roll(parts(block + 1), LANES - off, 1)
    return jnp.where(lane < LANES - off, a, b)


def pick(table, idx):
    return jnp.take_along_axis(table, idx, axis=1, mode="promise_in_bounds")


def kernel(factor_ref, ext_ref, off_ref, out_ref, words, offs, inv, wind, frac, res):
    fields, rows_ext, levels, _ = ext_ref.shape
    _, rows, _, cols = out_ref.shape
    count = words.shape[2]
    lane = lax.broadcasted_iota(jnp.int32, (levels, LANES), 1)
    blocks = cols // LANES + 2

    def block_of(ref, *lead):
        return lambda i: ref[(*lead, slice(None), slice(i * LANES, (i + 1) * LANES))]

    for f in range(fields):
        def biggest(r, top):
            for i in range(blocks):
                top = jnp.maximum(top, jnp.abs(block_of(ext_ref, f, r)(i).astype(jnp.float32)))
            return top

        top = lax.fori_loop(0, rows_ext, biggest, jnp.zeros((levels, LANES), jnp.float32))
        top = jnp.maximum(jnp.max(top, axis=1, keepdims=True), 1e-30)
        power = jnp.floor(jnp.log(32000.0 / top) * (1.0 / math.log(2.0)))
        scale = jnp.broadcast_to(jnp.exp(power * math.log(2.0)), (levels, LANES))
        inv[f] = (1.0 / 65536.0) / scale

        def pack(r, _):
            def quantized(i):
                v = block_of(ext_ref, f, r)(i).astype(jnp.float32)
                return jnp.floor(v * scale + 0.5).astype(jnp.int32)

            memo = {}

            def part(i):
                if i not in memo:
                    memo[i] = quantized(i)
                return memo[i]

            for j in range(count):
                q = window(part, LANES - HO + STEP * j, lane)
                words[f, r, j] = (q << 16) + pltpu.roll(q, LANES - 1, 1)
            return 0

        lax.fori_loop(0, rows_ext, pack, 0)

    def windows_of(y, _):
        for c in range(2):
            for j in range(count):
                offs[c, y, j] = window(block_of(off_ref, c, y), LANES - HO + STEP * j, lane)
        return 0

    lax.fori_loop(0, rows, windows_of, 0)

    sy, dy, dx = factor_ref[rows], factor_ref[rows + 1], factor_ref[rows + 2]

    def gathered(f, row, j, idx, groups, masks, k):
        value = pick(words[f, row + k, j], idx)
        for g in range(1, groups):
            value = jnp.where(masks[k][g - 1], pick(words[f, row + 4 * g + k, j], idx), value)
        return value

    def split(value):
        return value.astype(jnp.float32), (value << 16).astype(jnp.float32)

    def place(i):
        y = i // count
        return y, i - y * count

    def gather_wind(p):
        def step(i, _):
            y, j = place(i)
            groups, _ = classes((offs[0, y, j] >> 1) + 4)
            masks = [[groups[k] >= g for g in (1, 2)] for k in range(4)]
            idx = (lane + (offs[1, y, j] >> 1) + (2 * p - 1)) & (LANES - 1)
            for f in range(2):
                for k in range(4):
                    wind[i, f, k, p] = gathered(f, y + 5, j, idx, 3, masks, k)
            return 0

        lax.fori_loop(0, rows * count, step, 0)

    def trajectory(i, _):
        y, j = place(i)
        oy = offs[0, y, j]
        ox = offs[1, y, j]
        oyf = oy.astype(jnp.float32)
        oxf = ox.astype(jnp.float32)
        _, taps = classes((oy >> 1) + 4)
        stencils = [
            [[v for p in range(2) for v in split(wind[i, f, k, p])] for k in range(4)]
            for f in range(2)
        ]
        sx = factor_ref[y]
        odd_y = (oy & 1).astype(jnp.float32)
        odd_x = (ox & 1).astype(jnp.float32)
        fy = jnp.full(oy.shape, 0.5, jnp.float32)
        fx = fy
        for _ in range(ITERS):
            cw = col_weights((odd_x + fx) * 0.5)
            rw = class_weights(taps, (odd_y + fy) * 0.5)
            mid = []
            for f in range(2):
                total = 0.0
                for k in range(4):
                    v = stencils[f][k]
                    total += rw[k] * (cw[0] * v[0] + cw[1] * v[1] + cw[2] * v[2] + cw[3] * v[3])
                mid.append(total * inv[f])
            lx = dx * jnp.tanh(mid[0] * sx)
            ly = dy * jnp.tanh(mid[1] * sy)
            fy = 0.5 + 0.5 * jnp.tanh(0.5 * (ly - oyf - 0.5))
            fx = 0.5 + 0.5 * jnp.tanh(0.5 * (lx - oxf - 0.5))
        frac[i, 0] = fy
        frac[i, 1] = fx
        return 0

    def advect(p):
        def step(i, _):
            y, j = place(i)
            oy = offs[0, y, j]
            idx = (lane + offs[1, y, j] + (2 * p - 1)) & (LANES - 1)
            groups, taps = classes(oy + 8)
            masks = [[groups[k] >= g for g in (1, 2, 3, 4)] for k in range(4)]
            cw = col_weights(frac[i, 1])[2 * p : 2 * p + 2]
            rw = class_weights(taps, frac[i, 0])
            for f in range(fields):
                total = 0.0
                for k in range(4):
                    a, b = split(gathered(f, y + 1, j, idx, 5, masks, k))
                    total += rw[k] * (cw[0] * a + cw[1] * b)
                total = total * inv[f]
                res[f, y, j] = total if p == 0 else res[f, y, j] + total
            return 0

        lax.fori_loop(0, rows * count, step, 0)

    gather_wind(0)
    gather_wind(1)
    lax.fori_loop(0, rows * count, trajectory, 0)
    advect(0)
    advect(1)

    def merge(y, _):
        for f in range(fields):
            for m in range(cols // LANES):
                begin = m * LANES
                out = None
                for j in range(begin // STEP, (begin + LANES - 1) // STEP + 1):
                    moved = pltpu.roll(res[f, y, j], (STEP * j - HO - begin) % LANES, 1)
                    out = moved if out is None else jnp.where(lane >= STEP * j - begin, moved, out)
                out_ref[f, y, :, begin : begin + LANES] = out.astype(out_ref.dtype)
        return 0

    lax.fori_loop(0, rows, merge, 0)


def extend(fields):
    f, rows, levels, cols = fields.shape
    below = passed_along(fields[:, rows - HL :], "lat", 1)
    above = passed_along(fields[:, :HL], "lat", -1)
    tall = jnp.concatenate([below, fields, above], axis=1)
    count = rows + 2 * HL
    west_edge = jnp.moveaxis(tall[..., :HO], 3, 0).reshape(HO, f * count * levels)
    east_edge = jnp.moveaxis(tall[..., cols - HO :], 3, 0).reshape(HO, f * count * levels)
    west = from_behind(east_edge, "lon", 1).reshape(HO, f, count, levels)
    east = from_behind(west_edge, "lon", -1).reshape(HO, f, count, levels)
    blank = jnp.zeros((f, count, levels, LANES - HO), fields.dtype)
    return jnp.concatenate(
        [blank, jnp.moveaxis(west, 0, 3), tall, jnp.moveaxis(east, 0, 3), blank], axis=3
    )


def on_device(prognostic, halo_depth, cell_offsets):
    fields, levels, rows, cols = prognostic.shape
    ext = extend(jnp.transpose(prognostic, (0, 2, 1, 3)))
    off = jnp.pad(
        jnp.transpose(cell_offsets, (0, 2, 1, 3)), ((0, 0), (0, 0), (0, 0), (LANES, LANES))
    )
    lat_total = rows * lax.axis_size("lat")
    lat_index = (lax.axis_index("lat") * rows + jnp.arange(rows, dtype=jnp.int32)).astype(jnp.float32)
    coslat = jnp.cos((lat_index + 0.5) * (math.pi / lat_total) - 0.5 * math.pi)
    depth = halo_depth[:, 0, 0].astype(jnp.float32) - 1.0
    factor = jnp.concatenate(
        [-courant / (coslat * depth[1]), (-courant / depth[0])[None], depth]
    )
    count = -(-cols // STEP)
    moved = pl.pallas_call(
        kernel,
        out_shape=jax.ShapeDtypeStruct((fields, rows, levels, cols), jnp.bfloat16),
        in_specs=[
            pl.BlockSpec(memory_space=pltpu.SMEM),
            pl.BlockSpec(memory_space=pltpu.VMEM),
            pl.BlockSpec(memory_space=pltpu.VMEM),
        ],
        out_specs=pl.BlockSpec(memory_space=pltpu.VMEM),
        scratch_shapes=[
            pltpu.VMEM((fields, rows + 2 * HL, count, levels, LANES), jnp.int32),
            pltpu.VMEM((2, rows, count, levels, LANES), jnp.int32),
            pltpu.VMEM((fields, levels, LANES), jnp.float32),
            pltpu.VMEM((rows * count, 2, 4, 2, levels, LANES), jnp.int32),
            pltpu.VMEM((rows * count, 2, levels, LANES), jnp.float32),
            pltpu.VMEM((fields, rows, count, levels, LANES), jnp.float32),
        ],
        compiler_params=pltpu.CompilerParams(vmem_limit_bytes=40 * 2**20),
    )(factor, ext, off)
    return jnp.transpose(moved, (0, 2, 1, 3))


def solution(mesh):
    in_specs = (P(None, None, "lat", "lon"), P(None, "lat", "lon"), P(None, None, "lat", "lon"))
    out_specs = P(None, None, "lat", "lon")
    return jax.shard_map(
        on_device, mesh=mesh, in_specs=in_specs, out_specs=out_specs, check_vma=False
    )
```

```python
import functools
import math

import jax
import jax.numpy as jnp
from jax import lax
from jax.experimental import pallas as pl
from jax.experimental.pallas import tpu as pltpu
from jax.sharding import PartitionSpec as P

HO = 8
HL = 10
ITERS = 3
STEP = 104
LANES = 128
courant = 2.0


def passed_along(value, axis, by):
    devices = lax.axis_size(axis)
    pairs = [(i, i + by) for i in range(devices) if 0 <= i + by < devices]
    return lax.ppermute(value, axis, pairs)


def from_behind(value, axis, steps):
    count = lax.axis_size(axis)
    pairs = [(source, (source + steps) % count) for source in range(count)]
    return lax.ppermute(value, axis, pairs)


def far(m):
    return ((-0.5 * m + 2.5) * m - 4.0) * m + 2.0


def near(m):
    return (1.5 * m - 2.5) * m * m + 1.0


def tap_weights(g):
    return [far(1.0 + g), near(g), near(1.0 - g), far(2.0 - g)]


def col_weights(h):
    w = [v.astype(jnp.bfloat16).astype(jnp.float32) for v in tap_weights(h)]
    tiny = 1.0 / 65536.0
    return [w[0], w[1] - w[0] * tiny, w[2], w[3] - w[2] * tiny]


def classes(start):
    groups = [(start + (3 - k)) >> 2 for k in range(4)]
    taps = [(groups[k] << 2) + k - start for k in range(4)]
    return groups, taps


def class_weights(taps, g):
    w = tap_weights(g)
    return [
        jnp.where(t == 0, w[0], jnp.where(t == 1, w[1], jnp.where(t == 2, w[2], w[3])))
        for t in taps
    ]


def window(parts, first, lane):
    block, off = divmod(first, LANES)
    if off == 0:
        return parts(block)
    a = pltpu.roll(parts(block), LANES - off, 1)
    b = pltpu.roll(parts(block + 1), LANES - off, 1)
    return jnp.where(lane < LANES - off, a, b)


def pick(table, idx):
    return jnp.take_along_axis(table, idx, axis=1, mode="promise_in_bounds")


def kernel(factor_ref, west_ref, ext_ref, east_ref, off_ref, out_ref, words, offs, inv, res):
    fields, rows_ext, levels, _ = ext_ref.shape
    _, rows, _, cols = out_ref.shape
    count = words.shape[2]
    lane = lax.broadcasted_iota(jnp.int32, (levels, LANES), 1)
    blocks = cols // LANES + 2

    def block_of(f, r):
        def block(i):
            if i == 0:
                return west_ref[f, r]
            if i == blocks - 1:
                return east_ref[f, r]
            return ext_ref[f, r, :, (i - 1) * LANES : i * LANES]

        return block

    def offsets_of(c, y):
        def block(i):
            i = min(max(i, 1), blocks - 2)
            return off_ref[c, y, :, (i - 1) * LANES : i * LANES]

        return block

    for f in range(fields):
        def biggest(r, top):
            for i in range(blocks):
                top = jnp.maximum(top, jnp.abs(block_of(f, r)(i).astype(jnp.float32)))
            return top

        top = lax.fori_loop(0, rows_ext, biggest, jnp.zeros((levels, LANES), jnp.float32))
        top = jnp.maximum(jnp.max(top, axis=1, keepdims=True), 1e-30)
        power = jnp.floor(jnp.log(32000.0 / top) * (1.0 / math.log(2.0)))
        scale = jnp.broadcast_to(jnp.exp(power * math.log(2.0)), (levels, LANES))
        inv[f] = (1.0 / 65536.0) / scale

        def pack(r, _):
            def quantized(i):
                v = block_of(f, r)(i).astype(jnp.float32)
                return jnp.floor(v * scale + 0.5).astype(jnp.int32)

            memo = {}

            def part(i):
                if i not in memo:
                    memo[i] = quantized(i)
                return memo[i]

            for j in range(count):
                q = window(part, LANES - HO + STEP * j, lane)
                words[f, r, j] = (q << 16) + pltpu.roll(q, LANES - 1, 1)
            return 0

        lax.fori_loop(0, rows_ext, pack, 0)

    def windows_of(y, _):
        for c in range(2):
            for j in range(count):
                offs[c, y, j] = window(offsets_of(c, y), LANES - HO + STEP * j, lane)
        return 0

    lax.fori_loop(0, rows, windows_of, 0)

    sy, dy, dx = factor_ref[rows], factor_ref[rows + 1], factor_ref[rows + 2]

    def stencil(f, row, j, idx, groups, masks, k, p):
        value = pick(words[f, row + k, j], idx[p])
        for g in range(1, groups):
            value = jnp.where(masks[k][g - 1], pick(words[f, row + 4 * g + k, j], idx[p]), value)
        return value.astype(jnp.float32), (value << 16).astype(jnp.float32)

    def point(i, _):
        y = i // count
        j = i - y * count
        oy = offs[0, y, j]
        ox = offs[1, y, j]
        oyf = oy.astype(jnp.float32)
        oxf = ox.astype(jnp.float32)
        my = oy >> 1
        mx = ox >> 1
        idx = [(lane + mx + (2 * p - 1)) & (LANES - 1) for p in range(2)]
        groups, taps = classes(my + 4)
        masks = [[groups[k] >= g for g in (1, 2)] for k in range(4)]
        wind = [
            [
                [v for p in range(2) for v in stencil(f, y + 5, j, idx, 3, masks, k, p)]
                for k in range(4)
            ]
            for f in range(2)
        ]
        sx = factor_ref[y]
        odd_y = (oy & 1).astype(jnp.float32)
        odd_x = (ox & 1).astype(jnp.float32)
        fy = jnp.full(oy.shape, 0.5, jnp.float32)
        fx = fy
        for _ in range(ITERS):
            cw = col_weights((odd_x + fx) * 0.5)
            rw = class_weights(taps, (odd_y + fy) * 0.5)
            mid = []
            for f in range(2):
                total = 0.0
                for k in range(4):
                    v = wind[f][k]
                    total += rw[k] * (cw[0] * v[0] + cw[1] * v[1] + cw[2] * v[2] + cw[3] * v[3])
                mid.append(total * inv[f])
            lx = dx * jnp.tanh(mid[0] * sx)
            ly = dy * jnp.tanh(mid[1] * sy)
            fy = 0.5 + 0.5 * jnp.tanh(0.5 * (ly - oyf - 0.5))
            fx = 0.5 + 0.5 * jnp.tanh(0.5 * (lx - oxf - 0.5))

        idx = [(lane + ox + (2 * p - 1)) & (LANES - 1) for p in range(2)]
        groups, taps = classes(oy + 8)
        masks = [[groups[k] >= g for g in (1, 2, 3, 4)] for k in range(4)]
        cw = col_weights(fx)
        rw = class_weights(taps, fy)
        for f in range(fields):
            total = 0.0
            for k in range(4):
                a = stencil(f, y + 1, j, idx, 5, masks, k, 0)
                b = stencil(f, y + 1, j, idx, 5, masks, k, 1)
                total += rw[k] * (cw[0] * a[0] + cw[1] * a[1] + cw[2] * b[0] + cw[3] * b[1])
            res[f, y, j] = total * inv[f]
        return 0

    lax.fori_loop(0, rows * count, point, 0)

    def merge(y, _):
        for f in range(fields):
            for m in range(cols // LANES):
                begin = m * LANES
                out = None
                for j in range(begin // STEP, (begin + LANES - 1) // STEP + 1):
                    moved = pltpu.roll(res[f, y, j], (STEP * j - HO - begin) % LANES, 1)
                    out = moved if out is None else jnp.where(lane >= STEP * j - begin, moved, out)
                out_ref[f, y, :, begin : begin + LANES] = out.astype(out_ref.dtype)
        return 0

    lax.fori_loop(0, rows, merge, 0)


def extend(fields):
    f, rows, levels, cols = fields.shape
    below = passed_along(fields[:, rows - HL :], "lat", 1)
    above = passed_along(fields[:, :HL], "lat", -1)
    tall = jnp.concatenate([below, fields, above], axis=1)
    west = from_behind(tall[..., cols - LANES :], "lon", 1)
    east = from_behind(tall[..., :LANES], "lon", -1)
    return west, tall, east


def on_device(prognostic, halo_depth, cell_offsets):
    fields, levels, rows, cols = prognostic.shape
    west, tall, east = extend(jnp.transpose(prognostic, (0, 2, 1, 3)))
    off = jnp.transpose(cell_offsets, (0, 2, 1, 3))
    lat_total = rows * lax.axis_size("lat")
    lat_index = (lax.axis_index("lat") * rows + jnp.arange(rows, dtype=jnp.int32)).astype(jnp.float32)
    coslat = jnp.cos((lat_index + 0.5) * (math.pi / lat_total) - 0.5 * math.pi)
    depth = halo_depth[:, 0, 0].astype(jnp.float32) - 1.0
    factor = jnp.concatenate(
        [-courant / (coslat * depth[1]), (-courant / depth[0])[None], depth]
    )
    count = -(-cols // STEP)
    moved = pl.pallas_call(
        kernel,
        out_shape=jax.ShapeDtypeStruct((fields, rows, levels, cols), jnp.bfloat16),
        in_specs=[
            pl.BlockSpec(memory_space=pltpu.SMEM),
            pl.BlockSpec(memory_space=pltpu.VMEM),
            pl.BlockSpec(memory_space=pltpu.VMEM),
            pl.BlockSpec(memory_space=pltpu.VMEM),
            pl.BlockSpec(memory_space=pltpu.VMEM),
        ],
        out_specs=pl.BlockSpec(memory_space=pltpu.VMEM),
        scratch_shapes=[
            pltpu.VMEM((fields, rows + 2 * HL, count, levels, LANES), jnp.int32),
            pltpu.VMEM((2, rows, count, levels, LANES), jnp.int32),
            pltpu.VMEM((fields, levels, LANES), jnp.float32),
            pltpu.VMEM((fields, rows, count, levels, LANES), jnp.float32),
        ],
        compiler_params=pltpu.CompilerParams(vmem_limit_bytes=40 * 2**20),
    )(factor, west, tall, east, off)
    return jnp.transpose(moved, (0, 2, 1, 3))


def solution(mesh):
    in_specs = (P(None, None, "lat", "lon"), P(None, "lat", "lon"), P(None, None, "lat", "lon"))
    out_specs = P(None, None, "lat", "lon")
    return jax.shard_map(
        on_device, mesh=mesh, in_specs=in_specs, out_specs=out_specs, check_vma=False
    )
```

```python
import functools
import math

import jax
import jax.numpy as jnp
from jax import lax
from jax.experimental import pallas as pl
from jax.experimental.pallas import tpu as pltpu
from jax.sharding import PartitionSpec as P

HO = 8
HL = 10
ITERS = 3
STEP = 104
LANES = 128
courant = 2.0


def passed_along(value, axis, by):
    devices = lax.axis_size(axis)
    pairs = [(i, i + by) for i in range(devices) if 0 <= i + by < devices]
    return lax.ppermute(value, axis, pairs)


def from_behind(value, axis, steps):
    count = lax.axis_size(axis)
    pairs = [(source, (source + steps) % count) for source in range(count)]
    return lax.ppermute(value, axis, pairs)


def far(m):
    return ((-0.5 * m + 2.5) * m - 4.0) * m + 2.0


def near(m):
    return (1.5 * m - 2.5) * m * m + 1.0


def tap_weights(g):
    return [far(1.0 + g), near(g), near(1.0 - g), far(2.0 - g)]


def col_weights(h):
    w = [v.astype(jnp.bfloat16).astype(jnp.float32) for v in tap_weights(h)]
    tiny = 1.0 / 65536.0
    return [w[0], w[1] - w[0] * tiny, w[2], w[3] - w[2] * tiny]


def classes(start):
    groups = [(start + (3 - k)) >> 2 for k in range(4)]
    taps = [(groups[k] << 2) + k - start for k in range(4)]
    return groups, taps


def class_weights(taps, g):
    w = tap_weights(g)
    return [
        jnp.where(t == 0, w[0], jnp.where(t == 1, w[1], jnp.where(t == 2, w[2], w[3])))
        for t in taps
    ]


def window(parts, first, lane):
    block, off = divmod(first, LANES)
    if off == 0:
        return parts(block)
    a = pltpu.roll(parts(block), LANES - off, 1)
    b = pltpu.roll(parts(block + 1), LANES - off, 1)
    return jnp.where(lane < LANES - off, a, b)


def pick(table, idx):
    return jnp.take_along_axis(table, idx, axis=1, mode="promise_in_bounds")


def kernel(factor_ref, west_ref, ext_ref, east_ref, off_ref, out_ref, words, offs, inv, res):
    fields, rows_ext, levels, _ = ext_ref.shape
    _, rows, _, cols = out_ref.shape
    count = words.shape[2]
    lane = lax.broadcasted_iota(jnp.int32, (levels, LANES), 1)
    blocks = cols // LANES + 2

    def block_of(f, r):
        def block(i):
            if i == 0:
                return west_ref[f, r]
            if i == blocks - 1:
                return east_ref[f, r]
            return ext_ref[f, r, :, (i - 1) * LANES : i * LANES]

        return block

    def offsets_of(c, y):
        def block(i):
            i = min(max(i, 1), blocks - 2)
            return off_ref[c, y, :, (i - 1) * LANES : i * LANES]

        return block

    for f in range(fields):
        def biggest(r, top):
            for i in range(blocks):
                top = jnp.maximum(top, jnp.abs(block_of(f, r)(i).astype(jnp.float32)))
            return top

        top = lax.fori_loop(0, rows_ext, biggest, jnp.zeros((levels, LANES), jnp.float32))
        top = jnp.maximum(jnp.max(top, axis=1, keepdims=True), 1e-30)
        power = jnp.floor(jnp.log(32000.0 / top) * (1.0 / math.log(2.0)))
        scale = jnp.broadcast_to(jnp.exp(power * math.log(2.0)), (levels, LANES))
        inv[f] = (1.0 / 65536.0) / scale

        def pack(r, _):
            def quantized(i):
                v = block_of(f, r)(i).astype(jnp.float32)
                return jnp.floor(v * scale + 0.5).astype(jnp.int32)

            memo = {}

            def part(i):
                if i not in memo:
                    memo[i] = quantized(i)
                return memo[i]

            for j in range(count):
                q = window(part, LANES - HO + STEP * j, lane)
                words[f, r, j] = (q << 16) + pltpu.roll(q, LANES - 1, 1)
            return 0

        lax.fori_loop(0, rows_ext, pack, 0)

    def windows_of(y, _):
        for c in range(2):
            for j in range(count):
                offs[c, y, j] = window(offsets_of(c, y), LANES - HO + STEP * j, lane)
        return 0

    lax.fori_loop(0, rows, windows_of, 0)

    sy, dy, dx = factor_ref[rows], factor_ref[rows + 1], factor_ref[rows + 2]

    def stencil(f, row, j, idx, groups, masks, k, p):
        value = pick(words[f, row + k, j], idx[p])
        for g in range(1, groups):
            value = jnp.where(masks[k][g - 1], pick(words[f, row + 4 * g + k, j], idx[p]), value)
        return value.astype(jnp.float32), (value << 16).astype(jnp.float32)

    def point(i, _):
        y = i // count
        j = i - y * count
        oy = offs[0, y, j]
        ox = offs[1, y, j]
        oyf = oy.astype(jnp.float32)
        oxf = ox.astype(jnp.float32)
        my = oy >> 1
        mx = ox >> 1
        idx = [(lane + mx + (2 * p - 1)) & (LANES - 1) for p in range(2)]
        groups, taps = classes(my + 4)
        masks = [[groups[k] >= g for g in (1, 2)] for k in range(4)]
        wind = [
            [
                [v for p in range(2) for v in stencil(f, y + 5, j, idx, 3, masks, k, p)]
                for k in range(4)
            ]
            for f in range(2)
        ]
        sx = factor_ref[y]
        odd_y = (oy & 1).astype(jnp.float32)
        odd_x = (ox & 1).astype(jnp.float32)
        fy = jnp.full(oy.shape, 0.5, jnp.float32)
        fx = fy
        for _ in range(ITERS):
            cw = col_weights((odd_x + fx) * 0.5)
            rw = class_weights(taps, (odd_y + fy) * 0.5)
            mid = []
            for f in range(2):
                total = 0.0
                for k in range(4):
                    v = wind[f][k]
                    total += rw[k] * (cw[0] * v[0] + cw[1] * v[1] + cw[2] * v[2] + cw[3] * v[3])
                mid.append(total * inv[f])
            lx = dx * jnp.tanh(mid[0] * sx)
            ly = dy * jnp.tanh(mid[1] * sy)
            fy = 0.5 + 0.5 * jnp.tanh(0.5 * (ly - oyf - 0.5))
            fx = 0.5 + 0.5 * jnp.tanh(0.5 * (lx - oxf - 0.5))

        idx = [(lane + ox + (2 * p - 1)) & (LANES - 1) for p in range(2)]
        groups, taps = classes(oy + 8)
        masks = [[groups[k] >= g for g in (1, 2, 3, 4)] for k in range(4)]
        cw = col_weights(fx)
        rw = class_weights(taps, fy)
        for f in range(fields):
            total = 0.0
            for k in range(4):
                a = stencil(f, y + 1, j, idx, 5, masks, k, 0)
                b = stencil(f, y + 1, j, idx, 5, masks, k, 1)
                total += rw[k] * (cw[0] * a[0] + cw[1] * a[1] + cw[2] * b[0] + cw[3] * b[1])
            res[f, y, j] = total * inv[f]
        return 0

    lax.fori_loop(0, rows * count, point, 0)

    def merge(y, _):
        for f in range(fields):
            for m in range(cols // LANES):
                begin = m * LANES
                out = None
                for j in range(begin // STEP, (begin + LANES - 1) // STEP + 1):
                    moved = pltpu.roll(res[f, y, j], (STEP * j - HO - begin) % LANES, 1)
                    out = moved if out is None else jnp.where(lane >= STEP * j - begin, moved, out)
                out_ref[f, y, :, begin : begin + LANES] = out.astype(out_ref.dtype)
        return 0

    lax.fori_loop(0, rows, merge, 0)


def extend(fields):
    f, rows, levels, cols = fields.shape
    below = passed_along(fields[:, rows - HL :], "lat", 1)
    above = passed_along(fields[:, :HL], "lat", -1)
    tall = jnp.concatenate([below, fields, above], axis=1)
    outer = jnp.concatenate([below, above], axis=1)

    def beside(lanes, steps):
        own = from_behind(fields[..., lanes], "lon", steps)
        halo = from_behind(outer[..., lanes], "lon", steps)
        return jnp.concatenate([halo[:, :HL], own, halo[:, HL:]], axis=1)

    west = beside(slice(cols - LANES, cols), 1)
    east = beside(slice(0, LANES), -1)
    return west, tall, east


def on_device(prognostic, halo_depth, cell_offsets):
    fields, levels, rows, cols = prognostic.shape
    west, tall, east = extend(jnp.transpose(prognostic, (0, 2, 1, 3)))
    off = jnp.transpose(cell_offsets, (0, 2, 1, 3))
    lat_total = rows * lax.axis_size("lat")
    lat_index = (lax.axis_index("lat") * rows + jnp.arange(rows, dtype=jnp.int32)).astype(jnp.float32)
    coslat = jnp.cos((lat_index + 0.5) * (math.pi / lat_total) - 0.5 * math.pi)
    depth = halo_depth[:, 0, 0].astype(jnp.float32) - 1.0
    factor = jnp.concatenate(
        [-courant / (coslat * depth[1]), (-courant / depth[0])[None], depth]
    )
    count = -(-cols // STEP)
    moved = pl.pallas_call(
        kernel,
        out_shape=jax.ShapeDtypeStruct((fields, rows, levels, cols), jnp.bfloat16),
        in_specs=[
            pl.BlockSpec(memory_space=pltpu.SMEM),
            pl.BlockSpec(memory_space=pltpu.VMEM),
            pl.BlockSpec(memory_space=pltpu.VMEM),
            pl.BlockSpec(memory_space=pltpu.VMEM),
            pl.BlockSpec(memory_space=pltpu.VMEM),
        ],
        out_specs=pl.BlockSpec(memory_space=pltpu.VMEM),
        scratch_shapes=[
            pltpu.VMEM((fields, rows + 2 * HL, count, levels, LANES), jnp.int32),
            pltpu.VMEM((2, rows, count, levels, LANES), jnp.int32),
            pltpu.VMEM((fields, levels, LANES), jnp.float32),
            pltpu.VMEM((fields, rows, count, levels, LANES), jnp.float32),
        ],
        compiler_params=pltpu.CompilerParams(vmem_limit_bytes=40 * 2**20),
    )(factor, west, tall, east, off)
    return jnp.transpose(moved, (0, 2, 1, 3))


def solution(mesh):
    in_specs = (P(None, None, "lat", "lon"), P(None, "lat", "lon"), P(None, None, "lat", "lon"))
    out_specs = P(None, None, "lat", "lon")
    return jax.shard_map(
        on_device, mesh=mesh, in_specs=in_specs, out_specs=out_specs, check_vma=False
    )
```

```python
import functools
import math

import jax
import jax.numpy as jnp
from jax import lax
from jax.experimental import pallas as pl
from jax.experimental.pallas import tpu as pltpu
from jax.sharding import PartitionSpec as P

HO = 8
HL = 10
ITERS = 3
STEP = 104
LANES = 128
courant = 2.0


def passed_along(value, axis, by):
    devices = lax.axis_size(axis)
    pairs = [(i, i + by) for i in range(devices) if 0 <= i + by < devices]
    return lax.ppermute(value, axis, pairs)


def from_behind(value, axis, steps):
    count = lax.axis_size(axis)
    pairs = [(source, (source + steps) % count) for source in range(count)]
    return lax.ppermute(value, axis, pairs)


def diagonal(value, lon_by, lat_by):
    lons, lats = lax.axis_size("lon"), lax.axis_size("lat")
    pairs = [
        (i * lats + j, (i + lon_by) % lons * lats + j + lat_by)
        for i in range(lons)
        for j in range(lats)
        if 0 <= j + lat_by < lats
    ]
    return lax.ppermute(value, ("lon", "lat"), pairs)


def far(m):
    return ((-0.5 * m + 2.5) * m - 4.0) * m + 2.0


def near(m):
    return (1.5 * m - 2.5) * m * m + 1.0


def tap_weights(g):
    return [far(1.0 + g), near(g), near(1.0 - g), far(2.0 - g)]


def col_weights(h):
    w = [v.astype(jnp.bfloat16).astype(jnp.float32) for v in tap_weights(h)]
    tiny = 1.0 / 65536.0
    return [w[0], w[1] - w[0] * tiny, w[2], w[3] - w[2] * tiny]


def classes(start):
    groups = [(start + (3 - k)) >> 2 for k in range(4)]
    taps = [(groups[k] << 2) + k - start for k in range(4)]
    return groups, taps


def class_weights(taps, g):
    w = tap_weights(g)
    return [
        jnp.where(t == 0, w[0], jnp.where(t == 1, w[1], jnp.where(t == 2, w[2], w[3])))
        for t in taps
    ]


def window(parts, first, lane):
    block, off = divmod(first, LANES)
    if off == 0:
        return parts(block)
    a = pltpu.roll(parts(block), LANES - off, 1)
    b = pltpu.roll(parts(block + 1), LANES - off, 1)
    return jnp.where(lane < LANES - off, a, b)


def pick(table, idx):
    return jnp.take_along_axis(table, idx, axis=1, mode="promise_in_bounds")


def kernel(factor_ref, west_ref, ext_ref, east_ref, off_ref, out_ref, words, offs, inv, res):
    fields, rows_ext, levels, _ = ext_ref.shape
    _, rows, _, cols = out_ref.shape
    count = words.shape[2]
    lane = lax.broadcasted_iota(jnp.int32, (levels, LANES), 1)
    blocks = cols // LANES + 2

    def block_of(f, r):
        def block(i):
            if i == 0:
                return west_ref[f, r]
            if i == blocks - 1:
                return east_ref[f, r]
            return ext_ref[f, r, :, (i - 1) * LANES : i * LANES]

        return block

    def offsets_of(c, y):
        def block(i):
            i = min(max(i, 1), blocks - 2)
            return off_ref[c, y, :, (i - 1) * LANES : i * LANES]

        return block

    for f in range(fields):
        def biggest(r, top):
            for i in range(blocks):
                top = jnp.maximum(top, jnp.abs(block_of(f, r)(i).astype(jnp.float32)))
            return top

        top = lax.fori_loop(0, rows_ext, biggest, jnp.zeros((levels, LANES), jnp.float32))
        top = jnp.maximum(jnp.max(top, axis=1, keepdims=True), 1e-30)
        power = jnp.floor(jnp.log(32000.0 / top) * (1.0 / math.log(2.0)))
        scale = jnp.broadcast_to(jnp.exp(power * math.log(2.0)), (levels, LANES))
        inv[f] = (1.0 / 65536.0) / scale

        def pack(r, _):
            def quantized(i):
                v = block_of(f, r)(i).astype(jnp.float32)
                return jnp.floor(v * scale + 0.5).astype(jnp.int32)

            memo = {}

            def part(i):
                if i not in memo:
                    memo[i] = quantized(i)
                return memo[i]

            for j in range(count):
                q = window(part, LANES - HO + STEP * j, lane)
                words[f, r, j] = (q << 16) + pltpu.roll(q, LANES - 1, 1)
            return 0

        lax.fori_loop(0, rows_ext, pack, 0)

    def windows_of(y, _):
        for c in range(2):
            for j in range(count):
                offs[c, y, j] = window(offsets_of(c, y), LANES - HO + STEP * j, lane)
        return 0

    lax.fori_loop(0, rows, windows_of, 0)

    sy, dy, dx = factor_ref[rows], factor_ref[rows + 1], factor_ref[rows + 2]

    def stencil(f, row, j, idx, groups, masks, k, p):
        value = pick(words[f, row + k, j], idx[p])
        for g in range(1, groups):
            value = jnp.where(masks[k][g - 1], pick(words[f, row + 4 * g + k, j], idx[p]), value)
        return value.astype(jnp.float32), (value << 16).astype(jnp.float32)

    def point(i, _):
        y = i // count
        j = i - y * count
        oy = offs[0, y, j]
        ox = offs[1, y, j]
        oyf = oy.astype(jnp.float32)
        oxf = ox.astype(jnp.float32)
        my = oy >> 1
        mx = ox >> 1
        idx = [(lane + mx + (2 * p - 1)) & (LANES - 1) for p in range(2)]
        groups, taps = classes(my + 4)
        masks = [[groups[k] >= g for g in (1, 2)] for k in range(4)]
        wind = [
            [
                [v for p in range(2) for v in stencil(f, y + 5, j, idx, 3, masks, k, p)]
                for k in range(4)
            ]
            for f in range(2)
        ]
        sx = factor_ref[y]
        odd_y = (oy & 1).astype(jnp.float32)
        odd_x = (ox & 1).astype(jnp.float32)
        fy = jnp.full(oy.shape, 0.5, jnp.float32)
        fx = fy
        for _ in range(ITERS):
            cw = col_weights((odd_x + fx) * 0.5)
            rw = class_weights(taps, (odd_y + fy) * 0.5)
            mid = []
            for f in range(2):
                total = 0.0
                for k in range(4):
                    v = wind[f][k]
                    total += rw[k] * (cw[0] * v[0] + cw[1] * v[1] + cw[2] * v[2] + cw[3] * v[3])
                mid.append(total * inv[f])
            lx = dx * jnp.tanh(mid[0] * sx)
            ly = dy * jnp.tanh(mid[1] * sy)
            fy = 0.5 + 0.5 * jnp.tanh(0.5 * (ly - oyf - 0.5))
            fx = 0.5 + 0.5 * jnp.tanh(0.5 * (lx - oxf - 0.5))

        idx = [(lane + ox + (2 * p - 1)) & (LANES - 1) for p in range(2)]
        groups, taps = classes(oy + 8)
        masks = [[groups[k] >= g for g in (1, 2, 3, 4)] for k in range(4)]
        cw = col_weights(fx)
        rw = class_weights(taps, fy)
        for f in range(fields):
            total = 0.0
            for k in range(4):
                a = stencil(f, y + 1, j, idx, 5, masks, k, 0)
                b = stencil(f, y + 1, j, idx, 5, masks, k, 1)
                total += rw[k] * (cw[0] * a[0] + cw[1] * a[1] + cw[2] * b[0] + cw[3] * b[1])
            res[f, y, j] = total * inv[f]
        return 0

    lax.fori_loop(0, rows * count, point, 0)

    def merge(y, _):
        for f in range(fields):
            for m in range(cols // LANES):
                begin = m * LANES
                out = None
                for j in range(begin // STEP, (begin + LANES - 1) // STEP + 1):
                    moved = pltpu.roll(res[f, y, j], (STEP * j - HO - begin) % LANES, 1)
                    out = moved if out is None else jnp.where(lane >= STEP * j - begin, moved, out)
                out_ref[f, y, :, begin : begin + LANES] = out.astype(out_ref.dtype)
        return 0

    lax.fori_loop(0, rows, merge, 0)


def extend(fields):
    f, rows, levels, cols = fields.shape
    below = passed_along(fields[:, rows - HL :], "lat", 1)
    above = passed_along(fields[:, :HL], "lat", -1)
    tall = jnp.concatenate([below, fields, above], axis=1)
    def beside(lanes, steps):
        edge = fields[..., lanes]
        own = from_behind(edge, "lon", steps)
        low = diagonal(edge[:, rows - HL :], steps, 1)
        high = diagonal(edge[:, :HL], steps, -1)
        return jnp.concatenate([low, own, high], axis=1)

    west = beside(slice(cols - LANES, cols), 1)
    east = beside(slice(0, LANES), -1)
    return west, tall, east


def on_device(prognostic, halo_depth, cell_offsets):
    fields, levels, rows, cols = prognostic.shape
    west, tall, east = extend(jnp.transpose(prognostic, (0, 2, 1, 3)))
    off = jnp.transpose(cell_offsets, (0, 2, 1, 3))
    lat_total = rows * lax.axis_size("lat")
    lat_index = (lax.axis_index("lat") * rows + jnp.arange(rows, dtype=jnp.int32)).astype(jnp.float32)
    coslat = jnp.cos((lat_index + 0.5) * (math.pi / lat_total) - 0.5 * math.pi)
    depth = halo_depth[:, 0, 0].astype(jnp.float32) - 1.0
    factor = jnp.concatenate(
        [-courant / (coslat * depth[1]), (-courant / depth[0])[None], depth]
    )
    count = -(-cols // STEP)
    moved = pl.pallas_call(
        kernel,
        out_shape=jax.ShapeDtypeStruct((fields, rows, levels, cols), jnp.bfloat16),
        in_specs=[
            pl.BlockSpec(memory_space=pltpu.SMEM),
            pl.BlockSpec(memory_space=pltpu.VMEM),
            pl.BlockSpec(memory_space=pltpu.VMEM),
            pl.BlockSpec(memory_space=pltpu.VMEM),
            pl.BlockSpec(memory_space=pltpu.VMEM),
        ],
        out_specs=pl.BlockSpec(memory_space=pltpu.VMEM),
        scratch_shapes=[
            pltpu.VMEM((fields, rows + 2 * HL, count, levels, LANES), jnp.int32),
            pltpu.VMEM((2, rows, count, levels, LANES), jnp.int32),
            pltpu.VMEM((fields, levels, LANES), jnp.float32),
            pltpu.VMEM((fields, rows, count, levels, LANES), jnp.float32),
        ],
        compiler_params=pltpu.CompilerParams(vmem_limit_bytes=40 * 2**20),
    )(factor, west, tall, east, off)
    return jnp.transpose(moved, (0, 2, 1, 3))


def solution(mesh):
    in_specs = (P(None, None, "lat", "lon"), P(None, "lat", "lon"), P(None, None, "lat", "lon"))
    out_specs = P(None, None, "lat", "lon")
    return jax.shard_map(
        on_device, mesh=mesh, in_specs=in_specs, out_specs=out_specs, check_vma=False
    )
```
